32 devices in a mesh: section: 4 (over z), node: 2 (over y), local: 4 (over x, core).
Axes of the slice: x: 2, y: 2, z: 4, core: 2. Of those that a mesh axis runs over, the one named last changes fastest.
Arguments:
- layer_input: bfloat16 [4, 320, 7168], P('section', 'node', 'local'), may hold values from -6 to 6
- out_grad: bfloat16 [4, 320, 7168], P('section', 'node', 'local'), may hold values from -1.796875 to 1.796875
- routes: int32 [4, 320, 1], P('section', 'node'), may hold values from 0 to 1; in each aligned block of 160 rows (0 to 159, 160 to 319, ..., all dimensions but the last counted through in order) at most 120 rows name the same one
- gates: bfloat16 [4, 320, 1], P('section', 'node'), may hold values from 0.049804688 to 1
- gate_weight: bfloat16 [4, 2, 7168, 1024], P('section', 'node', None, 'local'), may hold values from -0.0625 to 0.0625
- up_weight: bfloat16 [4, 2, 7168, 1024], P('section', 'node', None, 'local'), may hold values from -0.0625 to 0.0625
- down_weight: bfloat16 [4, 2, 1024, 7168], P('section', 'node', 'local'), may hold values from -0.1875 to 0.1875
Outputs:
- passed: bfloat16 [4, 320, 7168], P('section', 'node', 'local')
- gate_grad: float32 [4, 320, 1], P('section', 'node')
- gate_wgrad: bfloat16 [4, 2, 7168, 1024], P('section', 'node', None, 'local')
- up_wgrad: bfloat16 [4, 2, 7168, 1024], P('section', 'node', None, 'local')
- down_wgrad: bfloat16 [4, 2, 1024, 7168], P('section', 'node', 'local')
The draws below stay inside these ranges and needn't reach their ends.
Inputs may be any that keep to these rules, and one draw needn't show every extreme that they name: Within each aligned block of 160 tokens of one layer (the tokens of one node), a token's 1 routes name different experts and no expert is named by more than 120 routes of the block; in every draw some block names some expert exactly 120 times.
All inputs are finite; a program needn't handle non-finite values.
Results may differ from the reference program's by a relative error of at most 0.0065.
Values may be sent and summed in bfloat16 or wider, within the bound.
A program may use at most 192 MiB of HBM per device.

```python
import math
import jax
import jax.numpy as jnp
import numpy as np
from jax import lax

D = 7168
FE = 1024
TOK_NODE = 160
LAYERS = 4
EXPERTS = 2
TOKENS = 320
ROUTES = 1
CAP = 120
F_DEV = 256
N_NODE = 2
N_LOCAL = 4


def block_levels(own_key, shape, split, smallest, high):
    def one(dim, blocks):
        heights = jax.random.uniform(jax.random.fold_in(jax.random.fold_in(own_key, 6), dim), (blocks,), jnp.float32, smallest / len(split), high / len(split))
        return jnp.repeat(jnp.exp(heights), shape[dim] // blocks).reshape((-1,) + (1,) * (len(shape) - dim - 1))

    factor_of = one(*split[0])
    for cut in split[1:]:
        factor_of = factor_of * one(*cut)
    return factor_of


def routed_block(rng, own, number, rows, count, top, limit, lean):
    sequence = jax.random.permutation(rng, count)
    packed, common = shares(count, rows * top, limit, lean, True), shares(count, rows * top, limit, lean, False)
    places = jnp.arange(count)

    def named(tallies, turn):
        used = int((tallies > 0).sum())
        fixed = max(1, used // 4)
        shifted = fixed + (places - fixed + turn * (used - fixed)) % max(1, count - fixed)
        return jnp.zeros((count,), jnp.int32).at[sequence[jnp.where(places < fixed, places, shifted)]].set(jnp.asarray(tallies, jnp.int32))

    tallies = jnp.where(number % 4 == 0, named(packed, number // 4), named(common, number - number // 4 - 1))
    mixed = jax.random.permutation(jax.random.fold_in(own, 3), count)
    source_of, sink = mixed[0:count // 2 * 2:2], mixed[1:count // 2 * 2:2]
    margin = jnp.minimum(tallies[source_of] - 1, limit - tallies[sink]) // 2
    margin = jnp.where((source_of == sequence[0]) | (sink == sequence[0]) | (tallies[sink] == 0), 0, jnp.maximum(margin, 0))
    shifted = jax.random.randint(jax.random.fold_in(own, 4), (count // 2,), 0, 1 << 20) % (margin + 1)
    tallies = tallies.at[source_of].add(-shifted).at[sink].add(shifted)
    items = jnp.searchsorted(jnp.cumsum(tallies), jnp.arange(rows * top), side="right").astype(jnp.int32)
    listing = items.reshape(top, rows).T
    listing = listing[jax.random.permutation(jax.random.fold_in(own, 1), rows)]
    turn = jax.random.randint(jax.random.fold_in(own, 2), (rows, 1), 0, top)
    return jnp.take_along_axis(listing, (jnp.arange(top)[None, :] + turn) % top, axis=1)


def shares(number_of, total, bound, skew, full):
    portions = [(1 << 20) // math.isqrt(standing ** skew) + 1 for standing in range(1, number_of + 1)]
    largest = bound if full else min(bound, max(-(-total // number_of), total * portions[0] // sum(portions)))
    least = 1 if total - largest >= number_of - 1 else 0
    holding, spare = [largest] + [least] * (number_of - 1), total - largest - least * (number_of - 1)
    while spare > 0:
        candidates = [i for i in range(1, number_of) if holding[i] < largest] or [i for i in range(1, number_of) if holding[i] < bound]
        whole, left = sum([portions[i] for i in candidates]), spare
        for i in candidates:
            more = min(bound - holding[i], max(1, left * portions[i] // whole), spare)
            holding[i] = holding[i] + more
            spare = spare - more
    return np.array(holding)


def scatter_about(key, dims, deviation, reach, split=(), kind=jnp.bfloat16):
    loudness = block_levels(key, dims, split, -0.22, 0.18) if split else 1.0
    drawn = jax.random.normal(key, dims, jnp.float32) * deviation * loudness
    return jnp.minimum(jnp.maximum(drawn, -reach), reach).astype(kind)


def setup_inputs(seed: int = 0) -> dict:
    keys = jax.random.split(jax.random.key(seed), 8)
    layer_input = scatter_about(keys[0], (LAYERS, TOKENS, D), 1.0, 6.0, ((0, 4), (1, 2), (2, 4)))
    out_grad = scatter_about(keys[1], (LAYERS, TOKENS, D), 0.3, 1.796875, ((0, 4), (1, 2), (2, 4)))
    routes_keys = jax.random.split(jax.random.fold_in(keys[2], 1), LAYERS * TOKENS // TOK_NODE)
    routes_turns = jax.random.permutation(jax.random.fold_in(keys[2], 3), LAYERS * TOKENS // TOK_NODE)
    routes = jax.vmap(lambda own, number: routed_block(jax.random.fold_in(keys[2], 2), own, number, TOK_NODE, EXPERTS, ROUTES, CAP, 2))(routes_keys, routes_turns).reshape((LAYERS, TOKENS, ROUTES))
    gates = jnp.clip(jnp.exp(math.log(1.0) - 2.9996462 * jax.random.uniform(keys[3], (LAYERS, TOKENS, ROUTES), jnp.float32) ** block_levels(keys[3], (LAYERS, TOKENS, ROUTES), ((0, 4), (1, 2)), -0.2, 0.2)), 0.049804688, 1.0).astype(jnp.bfloat16)
    gate_weight = scatter_about(keys[4], (LAYERS, EXPERTS, D, FE), D ** -0.5, 0.0625, ((0, 4), (1, 2), (3, 4)))
    up_weight = scatter_about(keys[5], (LAYERS, EXPERTS, D, FE), D ** -0.5, 0.0625, ((0, 4), (1, 2), (3, 4)))
    down_weight = scatter_about(keys[6], (LAYERS, EXPERTS, FE, D), FE ** -0.5, 0.1875, ((0, 4), (1, 2), (2, 4)))
    return dict(layer_input=layer_input, out_grad=out_grad, routes=routes, gates=gates, gate_weight=gate_weight, up_weight=up_weight, down_weight=down_weight)


def expert_backward(rows_input, rows_grads, gate_row, w_gate, w_up, w_down):
    pre_gate = jnp.dot(rows_input, w_gate, preferred_element_type=jnp.float32)
    pre_up = jnp.dot(rows_input, w_up, preferred_element_type=jnp.float32)
    hidden_raw = jnp.dot(rows_grads, w_down.T, preferred_element_type=jnp.float32)
    sigmoid_gate = jax.nn.sigmoid(pre_gate)
    swish_gate = pre_gate * sigmoid_gate
    activation = swish_gate * pre_up
    group_gate = jnp.sum((activation * hidden_raw).reshape(-1, N_LOCAL, F_DEV), axis=2)
    group_gate = lax.optimization_barrier(group_gate.astype(jnp.bfloat16))
    gate_total = jnp.sum(group_gate.astype(jnp.float32), axis=1)
    gate_total = lax.optimization_barrier(gate_total.astype(jnp.bfloat16))
    gated_act = (gate_row[:, None] * activation).astype(jnp.bfloat16)
    scaled = gate_row[:, None] * hidden_raw
    grad_gate = (scaled * pre_up * sigmoid_gate * (1.0 + pre_gate * (1.0 - sigmoid_gate))).astype(jnp.bfloat16)
    grad_up = (scaled * swish_gate).astype(jnp.bfloat16)
    route_total = jnp.zeros((rows_input.shape[0], rows_input.shape[1]), jnp.float32)
    for group_index in range(N_LOCAL):
        first_unit = group_index * F_DEV
        last_unit = first_unit + F_DEV
        group_term = jnp.dot(grad_gate[:, first_unit:last_unit], w_gate[:, first_unit:last_unit].T, preferred_element_type=jnp.float32)
        group_term = group_term + jnp.dot(grad_up[:, first_unit:last_unit], w_up[:, first_unit:last_unit].T, preferred_element_type=jnp.float32)
        group_term = lax.optimization_barrier(group_term.astype(jnp.bfloat16))
        route_total = route_total + group_term.astype(jnp.float32)
    route_grad = lax.optimization_barrier(route_total.astype(jnp.bfloat16))
    gate_wgrad = jnp.dot(rows_input.T, grad_gate, preferred_element_type=jnp.float32).astype(jnp.bfloat16)
    up_wgrad = jnp.dot(rows_input.T, grad_up, preferred_element_type=jnp.float32).astype(jnp.bfloat16)
    down_wgrad = jnp.dot(gated_act.T, rows_grads, preferred_element_type=jnp.float32).astype(jnp.bfloat16)
    return gate_total, route_grad, gate_wgrad, up_wgrad, down_wgrad


def reference(layer_input, out_grad, routes, gates, gate_weight, up_weight, down_weight):
    entries = TOKENS * ROUTES
    slot_total = N_NODE * CAP
    input_layers = []
    gate_layers = []
    gate_wgrads = []
    up_wgrads = []
    down_wgrads = []
    for layer_index in range(LAYERS):
        flat_ids = routes[layer_index].reshape(entries).astype(jnp.int32)
        flat_gates = gates[layer_index].reshape(entries).astype(jnp.float32)
        inputs_now = layer_input[layer_index]
        grads_now = out_grad[layer_index]

        def one_expert(carry, pieces):
            grad_sum, gate_flat = carry
            w_gate, w_up, w_down, expert = pieces
            chosen = flat_ids == expert
            order_rank = (jnp.cumsum(chosen.astype(jnp.int32)) - 1).astype(jnp.int32)
            target = jnp.where(chosen, order_rank, slot_total).astype(jnp.int32)
            slot_table = jnp.full((slot_total,), entries, jnp.int32)
            slot_table = slot_table.at[target].set(jnp.arange(entries, dtype=jnp.int32), mode="drop")
            live_slots = slot_table < entries
            entry_idx = jnp.minimum(slot_table, entries - 1).astype(jnp.int32)
            token_idx = (entry_idx // ROUTES).astype(jnp.int32)
            live_scale = live_slots.astype(jnp.bfloat16)[:, None]
            rows_input = inputs_now[token_idx] * live_scale
            rows_grads = grads_now[token_idx] * live_scale
            gate_row = flat_gates[entry_idx] * live_slots.astype(jnp.float32)
            gate_total, route_grad, gate_wgrad, up_wgrad, down_wgrad = expert_backward(rows_input, rows_grads, gate_row, w_gate, w_up, w_down)
            grad_sum = grad_sum.at[slot_table].set(route_grad.astype(jnp.float32), mode="drop")
            gate_flat = gate_flat.at[slot_table].set(gate_total.astype(jnp.float32), mode="drop")
            return (grad_sum, gate_flat), (gate_wgrad, up_wgrad, down_wgrad)

        start = (jnp.zeros((entries, D), jnp.float32), jnp.zeros((entries,), jnp.float32))
        pieces = (gate_weight[layer_index], up_weight[layer_index], down_weight[layer_index], jnp.arange(EXPERTS, dtype=jnp.int32))
        (grad_sum, gate_flat), (gate_wgrad, up_wgrad, down_wgrad) = lax.scan(one_expert, start, pieces)
        input_layers.append(jnp.sum(grad_sum.reshape(TOKENS, ROUTES, D), axis=1).astype(jnp.bfloat16))
        gate_layers.append(gate_flat.reshape(TOKENS, ROUTES))
        gate_wgrads.append(gate_wgrad)
        up_wgrads.append(up_wgrad)
        down_wgrads.append(down_wgrad)
    passed = jnp.roll(jnp.stack(input_layers), -1, axis=0)
    return passed, jnp.stack(gate_layers), jnp.stack(gate_wgrads), jnp.stack(up_wgrads), jnp.stack(down_wgrads)
```

```python
import functools

import jax
import jax.numpy as jnp
from jax import lax
from jax.experimental import pallas as pl
from jax.experimental.pallas import tpu as pltpu
from jax.sharding import PartitionSpec as P

F32 = jnp.float32
BF16 = jnp.bfloat16
MESH = pl.DeviceIdType.MESH
NT = (((1,), (1,)), ((), ()))
TN = (((0,), (0,)), ((), ()))


def from_behind(value, axis, by):
    length = lax.axis_size(axis)
    return lax.ppermute(value, axis, [(i, (i + by) % length) for i in range(length)])


def slot_tables(route_ids, node_count, capacity):
    token_count, route_count = route_ids.shape
    entries = token_count * route_count
    flat_ids = route_ids.reshape(entries)
    order = jnp.arange(entries, dtype=jnp.int32)
    earlier = (order[None, :] < order[:, None]) & (flat_ids[None, :] == flat_ids[:, None])
    slot_of = jnp.sum(earlier.astype(jnp.int32), axis=1)
    slot_table = jnp.full((capacity, node_count), entries, jnp.int32)
    slot_table = slot_table.at[slot_of, flat_ids].set(order, mode="drop")
    return (slot_of, flat_ids, slot_table)


def general_body(layer_input, out_grad, routes, gates, gate_weight, up_weight, down_weight):
    node_count = lax.axis_size("node")
    local_count = lax.axis_size("local")
    token_count = layer_input.shape[1]
    quarter = layer_input.shape[2]
    route_count = routes.shape[2]
    capacity = min(2 * token_count * route_count // node_count, 3 * token_count // 4)
    entries = token_count * route_count
    slot_of, flat_ids, slot_table = slot_tables(routes[0], node_count, capacity)
    live_slots = slot_table < entries
    entry_idx = jnp.minimum(slot_table, entries - 1)
    token_idx = entry_idx // route_count
    live_scale = live_slots.astype(BF16)
    send_input = layer_input[0][token_idx] * live_scale[:, :, None]
    send_grads = out_grad[0][token_idx] * live_scale[:, :, None]
    send_gates = gates[0].reshape(entries)[entry_idx] * live_scale
    wide_shape = (capacity, node_count, local_count, quarter)

    def exchange(value):
        return lax.all_to_all(value, ("node", "local"), split_axis=1, concat_axis=1, tiled=True)

    def widen(value):
        wide = jnp.broadcast_to(value[:, :, None, :], wide_shape)
        return wide.reshape(capacity, node_count * local_count, quarter)

    wide_gates = jnp.broadcast_to(send_gates[:, :, None], wide_shape[:3])
    got_input = exchange(widen(send_input))
    got_grads = exchange(widen(send_grads))
    got_gates = exchange(wide_gates.reshape(capacity, node_count * local_count))
    row_total = capacity * node_count
    flat_input = got_input.reshape(row_total, -1)
    flat_grads = got_grads.reshape(row_total, -1)
    own_column = (jnp.arange(local_count, dtype=jnp.int32) == lax.axis_index("local")).astype(F32)
    gate_column = jnp.sum(
        got_gates.reshape(capacity, node_count, local_count).astype(F32) * own_column, axis=2
    ).reshape(row_total, 1)
    w_gate = gate_weight[0, 0]
    w_up = up_weight[0, 0]
    w_down = down_weight[0, 0]
    pre_gate = jnp.dot(flat_input, w_gate, preferred_element_type=F32)
    pre_up = jnp.dot(flat_input, w_up, preferred_element_type=F32)
    hidden_raw = jnp.dot(flat_grads, w_down.T, preferred_element_type=F32)
    gate_part, gated_act, grad_gate, grad_up = unit_math(pre_gate, pre_up, hidden_raw, gate_column)
    unit_terms = jnp.dot(grad_gate, w_gate.T, preferred_element_type=F32)
    unit_terms = unit_terms + jnp.dot(grad_up, w_up.T, preferred_element_type=F32)
    gate_spread = jnp.broadcast_to(gate_part.reshape(capacity, node_count, 1), wide_shape[:3])
    got_rows = exchange(unit_terms.astype(BF16).reshape(capacity, node_count * local_count, quarter))
    got_gate = exchange(gate_spread.astype(BF16).reshape(capacity, node_count * local_count))
    route_rows = jnp.sum(got_rows.reshape(wide_shape), axis=2, dtype=F32)
    route_rows = lax.optimization_barrier(route_rows.astype(BF16))
    route_gate = jnp.sum(got_gate.reshape(wide_shape[:3]), axis=2, dtype=F32)
    route_gate = lax.optimization_barrier(route_gate.astype(BF16))
    flat_rows = route_rows.reshape(row_total, quarter)
    position = jnp.minimum(slot_of * node_count + flat_ids, row_total - 1)
    per_entry = flat_rows[position].reshape(token_count, route_count, quarter)
    input_grad = jnp.sum(per_entry, axis=1, dtype=F32).astype(BF16)
    gate_grad = (
        route_gate.reshape(row_total)[position].astype(F32).reshape(1, token_count, route_count)
    )
    passed = from_behind(input_grad[None], "section", -1)
    gate_wgrad = jnp.dot(flat_input.T, grad_gate, preferred_element_type=F32).astype(BF16)
    up_wgrad = jnp.dot(flat_input.T, grad_up, preferred_element_type=F32).astype(BF16)
    down_wgrad = jnp.dot(gated_act.T, flat_grads, preferred_element_type=F32).astype(BF16)
    return (passed, gate_grad, gate_wgrad[None, None], up_wgrad[None, None], down_wgrad[None, None])


def unit_math(pre_gate, pre_up, hidden_raw, gate_column):
    sigmoid_gate = jax.nn.sigmoid(pre_gate)
    swish_gate = pre_gate * sigmoid_gate
    activation = swish_gate * pre_up
    gate_part = jnp.sum(activation * hidden_raw, axis=1, keepdims=True)
    gated_act = (gate_column * activation).astype(BF16)
    scaled = gate_column * hidden_raw
    grad_gate = (scaled * pre_up * sigmoid_gate * (1.0 + pre_gate * (1.0 - sigmoid_gate))).astype(
        BF16
    )
    grad_up = (scaled * swish_gate).astype(BF16)
    return gate_part, gated_act, grad_gate, grad_up


def layer_kernel(
    T, K, C, F,
    x_ref, dy_ref, routes_ref, gates_ref, wg_hbm, wu_hbm, wd_hbm,
    ig_ref, gate_out_ref, gg_ref, gu_ref, ga_ref, rx_hbm, rd_hbm,
    wg, wu, wd, pick, xf, rx, rd, xs, dys, gsend, grecv, pg, pu, hr,
    sa, ra, sb, rb, own, sc, rc, gts, gtr,
    send_sem, recv_sem, load_sem, out_sem,
):
    n = lax.axis_index("node")
    l = lax.axis_index("local")
    xi = l // 2
    ci = l % 2
    q_me = l
    q_xm = 2 * (1 - xi) + ci
    q_cm = 2 * xi + 1 - ci
    q_cx = 2 * (1 - xi) + 1 - ci
    x_mate = {"local": q_xm}
    c_mate = {"local": q_cm}
    y_mate = {"node": 1 - n}

    loads = [
        pltpu.make_async_copy(wg_hbm, wg, load_sem.at[0]),
        pltpu.make_async_copy(wu_hbm, wu, load_sem.at[1]),
    ]
    for q in range(4):
        loads.append(
            pltpu.make_async_copy(wd_hbm.at[:, pl.ds(q * C, C)], wd.at[q], load_sem.at[2 + q])
        )

    barrier = pltpu.get_barrier_semaphore()
    for dn in range(2):
        for dl in range(4):
            if dn or dl:
                pl.semaphore_signal(
                    barrier, inc=1, device_id_type=MESH,
                    device_id={"node": lax.rem(n + dn, 2), "local": lax.rem(l + dl, 4)},
                )
    pl.semaphore_wait(barrier, 7)

    sent = []

    def send(i, src, dst, dev):
        d = pltpu.make_async_remote_copy(
            src_ref=src, dst_ref=dst, send_sem=send_sem.at[i], recv_sem=recv_sem.at[i],
            device_id=dev, device_id_type=MESH,
        )
        d.start()
        sent.append(d)
        return d

    m0 = send(0, x_ref, xf.at[q_me], x_mate)

    ids = routes_ref[...]
    before = lax.broadcasted_iota(jnp.int32, (T, T), 0) < lax.broadcasted_iota(jnp.int32, (T, T), 1)
    before = jnp.where(before, 1.0, 0.0).astype(BF16)
    slot = lax.broadcasted_iota(jnp.int32, (K, T), 0).astype(F32)
    gate_row = gates_ref[...].astype(F32)
    columns = []
    for g in range(2):
        named = jnp.where(ids == (n if g == 0 else 1 - n), 1.0, 0.0)
        rank = jnp.dot(
            jnp.broadcast_to(named, (16, T)).astype(BF16), before, preferred_element_type=F32
        )[0:1]
        hit = jnp.where(rank == slot, jnp.broadcast_to(named, (K, T)), 0.0)
        pick[g] = hit.astype(BF16)
        columns.append(jnp.sum(hit * gate_row, axis=1, keepdims=True))

    def select(g, rows):
        return jnp.dot(pick[g], rows, preferred_element_type=F32).astype(BF16)

    dys[...] = select(1, dy_ref[...])
    m3 = send(3, dys, rd.at[q_me, 1], y_mate)
    gsend[...] = jnp.broadcast_to(columns[1], (K, 128)).astype(BF16)
    m14 = send(14, gsend, grecv, y_mate)
    rd[q_me, 0] = select(0, dy_ref[...])
    m4 = send(4, rd.at[q_me, 0], rd.at[q_me, 0], x_mate)
    xs[0] = select(1, x_ref[...])
    m10 = send(10, xs.at[0], rx.at[q_me, 1], y_mate)
    m5 = send(5, rd.at[q_me, 0], rd.at[q_me, 0], c_mate)
    m1 = send(1, x_ref, xf.at[q_me], c_mate)
    for d in loads:
        d.start()
    rx[q_me, 0] = select(0, x_ref[...])

    m0.wait_recv()
    xs[1] = select(1, xf[q_xm])
    m11 = send(11, xs.at[1], rx.at[q_xm, 1], y_mate)
    m2 = send(2, xf.at[q_xm], xf.at[q_xm], c_mate)
    m3.wait_recv()
    m7 = send(7, rd.at[q_me, 1], rd.at[q_me, 1], x_mate)
    m8 = send(8, rd.at[q_me, 1], rd.at[q_me, 1], c_mate)
    rx[q_xm, 0] = select(0, xf[q_xm])
    m1.wait_recv()
    rx[q_cm, 0] = select(0, xf[q_cm])
    m4.wait_recv()
    m6 = send(6, rd.at[q_xm, 0], rd.at[q_xm, 0], c_mate)
    m10.wait_recv()
    m12 = send(12, rx.at[q_me, 1], rx.at[q_me, 1], c_mate)
    m2.wait_recv()
    rx[q_cx, 0] = select(0, xf[q_cx])

    for d in loads:
        d.wait()
    pg[...] = jnp.zeros_like(pg)
    pu[...] = jnp.zeros_like(pu)
    hr[...] = jnp.zeros_like(hr)

    def project(q):
        rows = rx[q].reshape(2 * K, C)
        pg[...] += jnp.dot(rows, wg[q], preferred_element_type=F32)
        pu[...] += jnp.dot(rows, wu[q], preferred_element_type=F32)

    def hidden(q):
        rows = rd[q].reshape(2 * K, C)
        hr[...] += lax.dot_general(rows, wd[q], NT, preferred_element_type=F32)

    project(q_me)
    m12.wait_recv()
    project(q_cm)
    m5.wait_recv()
    m8.wait_recv()
    m6.wait_recv()
    hidden(q_me)
    hidden(q_cm)
    m7.wait_recv()
    m9 = send(9, rd.at[q_xm, 1], rd.at[q_xm, 1], c_mate)
    m11.wait_recv()
    m13 = send(13, rx.at[q_xm, 1], rx.at[q_xm, 1], c_mate)
    hidden(q_xm)
    project(q_xm)
    m9.wait_recv()
    hidden(q_cx)
    m13.wait_recv()
    project(q_cx)
    out_copies = [
        pltpu.make_async_copy(rx, rx_hbm, out_sem.at[0]),
        pltpu.make_async_copy(rd, rd_hbm, out_sem.at[1]),
    ]
    for d in out_copies:
        d.start()
    m14.wait_recv()

    parts = []
    for g in range(2):
        rows = pl.ds(g * K, K)
        column = columns[0] if g == 0 else grecv[:, 0:1].astype(F32)
        part, act, d_gate, d_up = unit_math(pg[rows], pu[rows], hr[rows], column)
        ga_ref[rows] = act
        gg_ref[rows] = d_gate
        gu_ref[rows] = d_up
        parts.append(part)

    def terms(q, store):
        @pl.loop(0, C // 256)
        def _(j):
            at = pl.ds(pl.multiple_of(j * 256, 256), 256)
            t = lax.dot_general(gg_ref[...], wg[q, at], NT, preferred_element_type=F32)
            t += lax.dot_general(gu_ref[...], wu[q, at], NT, preferred_element_type=F32)
            t = t.astype(BF16)
            for g in range(2):
                store[g, :, at] = t[g * K : (g + 1) * K]

    terms(q_cx, sa.at[0])
    a0 = send(15, sa.at[0], ra.at[0], c_mate)
    terms(q_xm, sb)
    a0.wait_recv()
    b = [None, None]
    for g in (1, 0):
        sb[g] = (sb[g].astype(F32) + ra[0, g].astype(F32)).astype(BF16)
        b[g] = send(17 + g, sb.at[g], rb.at[g], x_mate)
    terms(q_cm, sa.at[1])
    a1 = send(16, sa.at[1], ra.at[1], c_mate)
    terms(q_me, own)

    eye = lax.broadcasted_iota(jnp.int32, (K, K), 0) == lax.broadcasted_iota(jnp.int32, (K, K), 1)
    for g in range(2):
        part = parts[g].astype(BF16).astype(F32)
        row = jnp.sum(jnp.where(eye, part, 0.0), axis=0, keepdims=True)
        gts[g] = jnp.broadcast_to(row, (16, K)).astype(BF16)
    gtr[l] = gts[0]
    gate_sent = []
    for k in range(1, 4):
        gate_sent.append(send(20 + k, gts.at[0], gtr.at[l], {"local": lax.rem(l + k, 4)}))
    for k in range(4):
        gate_sent.append(
            send(24 + k, gts.at[1], gtr.at[4 + l], {"node": 1 - n, "local": lax.rem(l + k, 4)})
        )

    a1.wait_recv()
    b[1].wait_recv()
    sc[...] = (own[1].astype(F32) + ra[1, 1].astype(F32) + rb[1].astype(F32)).astype(BF16)
    c = send(19, sc, rc, y_mate)
    for d in gate_sent:
        d.wait_recv()
    total = jnp.zeros((16, T), F32)
    for g in range(2):
        row = gtr[4 * g].astype(F32)
        for k in range(1, 4):
            row += gtr[4 * g + k].astype(F32)
        total += jnp.dot(row.astype(BF16), pick[g], preferred_element_type=F32)
    gate_out_ref[...] = total[0:1]

    b[0].wait_recv()
    own[0] = (own[0].astype(F32) + ra[1, 0].astype(F32) + rb[0].astype(F32)).astype(BF16)
    c.wait_recv()

    @pl.loop(0, C // 256)
    def _(j):
        at = pl.ds(pl.multiple_of(j * 256, 256), 256)
        t = lax.dot_general(pick[0], own[0, :, at], TN, preferred_element_type=F32)
        t += lax.dot_general(pick[1], rc[:, at], TN, preferred_element_type=F32)
        ig_ref[:, at] = t.astype(BF16)

    for d in sent:
        d.wait_send()
    for d in out_copies:
        d.wait()


def wgrad_kernel(rx_ref, rd_ref, gg_ref, gu_ref, ga_ref, gw_ref, uw_ref, dw_ref):
    rows = rx_ref[0]
    gw_ref[...] = lax.dot_general(rows, gg_ref[...], TN, preferred_element_type=F32).astype(BF16)
    uw_ref[...] = lax.dot_general(rows, gu_ref[...], TN, preferred_element_type=F32).astype(BF16)
    dw_ref[...] = lax.dot_general(
        ga_ref[...], rd_ref[0], TN, preferred_element_type=F32
    ).astype(BF16)


def fused_body(layer_input, out_grad, routes, gates, gate_weight, up_weight, down_weight):
    T, C = layer_input.shape[1:]
    D, F = gate_weight.shape[2:]
    K = -(-(3 * T // 4) // 128) * 128
    vmem = pl.BlockSpec(memory_space=pltpu.VMEM)
    hbm = pl.BlockSpec(memory_space=pl.ANY)
    shape = jax.ShapeDtypeStruct
    rows = (4, 2, K, C)
    ig, gate_grad, gg, gu, ga, rx, rd = pl.pallas_call(
        functools.partial(layer_kernel, T, K, C, F),
        out_shape=(
            shape((T, C), BF16), shape((1, T), F32),
            shape((2 * K, F), BF16), shape((2 * K, F), BF16), shape((2 * K, F), BF16),
            shape(rows, BF16), shape(rows, BF16),
        ),
        in_specs=[vmem] * 4 + [hbm] * 3,
        out_specs=(vmem,) * 5 + (hbm,) * 2,
        scratch_shapes=[
            pltpu.VMEM((4, C, F), BF16), pltpu.VMEM((4, C, F), BF16), pltpu.VMEM((4, F, C), BF16),
            pltpu.VMEM((2, K, T), BF16), pltpu.VMEM((4, T, C), BF16),
            pltpu.VMEM(rows, BF16), pltpu.VMEM(rows, BF16),
            pltpu.VMEM((2, K, C), BF16), pltpu.VMEM((K, C), BF16),
            pltpu.VMEM((K, 128), BF16), pltpu.VMEM((K, 128), BF16),
            pltpu.VMEM((2 * K, F), F32), pltpu.VMEM((2 * K, F), F32), pltpu.VMEM((2 * K, F), F32),
            pltpu.VMEM((2, 2, K, C), BF16), pltpu.VMEM((2, 2, K, C), BF16),
            pltpu.VMEM((2, K, C), BF16), pltpu.VMEM((2, K, C), BF16), pltpu.VMEM((2, K, C), BF16),
            pltpu.VMEM((K, C), BF16), pltpu.VMEM((K, C), BF16),
            pltpu.VMEM((2, 16, K), BF16), pltpu.VMEM((8, 16, K), BF16),
            pltpu.SemaphoreType.DMA((28,)), pltpu.SemaphoreType.DMA((28,)),
            pltpu.SemaphoreType.DMA((6,)), pltpu.SemaphoreType.DMA((2,)),
        ],
        compiler_params=pltpu.CompilerParams(
            collective_id=0, has_side_effects=True, vmem_limit_bytes=52 * 2**20
        ),
        name="layer",
    )(
        layer_input[0], out_grad[0], routes.reshape(1, T), gates.reshape(1, T),
        gate_weight.reshape(4, C, F), up_weight.reshape(4, C, F), down_weight.reshape(F, D),
    )
    passed = from_behind(ig[None], "section", -1)
    half = C // 2
    slab = pl.BlockSpec((1, 2 * K, half), lambda i: (i // 2, 0, i % 2))
    units = pl.BlockSpec((2 * K, F), lambda i: (0, 0))
    tall = pl.BlockSpec((half, F), lambda i: (i, 0))
    wide = pl.BlockSpec((F, half), lambda i: (0, i))
    gw, uw, dw = pl.pallas_call(
        wgrad_kernel,
        grid=(8,),
        out_shape=(shape((D, F), BF16), shape((D, F), BF16), shape((F, D), BF16)),
        in_specs=[slab, slab, units, units, units],
        out_specs=(tall, tall, wide),
        compiler_params=pltpu.CompilerParams(vmem_limit_bytes=24 * 2**20),
        cost_estimate=pl.CostEstimate(
            flops=12 * K * D * F, bytes_accessed=8 * K * D + 6 * D * F, transcendentals=0
        ),
        name="wgrad",
    )(rx.reshape(4, 2 * K, C), rd.reshape(4, 2 * K, C), gg, gu, ga)
    return (
        passed, gate_grad.reshape(1, T, 1), gw[None, None], uw[None, None], dw[None, None]
    )


def body(*args):
    routes, gate_weight = args[2], args[4]
    small = lax.axis_size("node") == 2 and lax.axis_size("local") == 4
    if small and routes.shape[2] == 1 and gate_weight.shape[1] == 1:
        return fused_body(*args)
    return general_body(*args)


def solution(mesh):
    return jax.shard_map(
        body,
        mesh=mesh,
        in_specs=(
            P("section", "node", "local"),
            P("section", "node", "local"),
            P("section", "node", None),
            P("section", "node", None),
            P("section", "node", None, "local"),
            P("section", "node", None, "local"),
            P("section", "node", "local", None),
        ),
        out_specs=(
            P("section", "node", "local"),
            P("section", "node", None),
            P("section", "node", None, "local"),
            P("section", "node", None, "local"),
            P("section", "node", "local", None),
        ),
        check_vma=False,
    )
```

```python
import functools

import jax
import jax.numpy as jnp
from jax import lax
from jax.experimental import pallas as pl
from jax.experimental.pallas import tpu as pltpu
from jax.sharding import PartitionSpec as P

F32 = jnp.float32
BF16 = jnp.bfloat16
MESH = pl.DeviceIdType.MESH
NT = (((1,), (1,)), ((), ()))
TN = (((0,), (0,)), ((), ()))


def from_behind(value, axis, by):
    length = lax.axis_size(axis)
    return lax.ppermute(value, axis, [(i, (i + by) % length) for i in range(length)])


def slot_tables(route_ids, node_count, capacity):
    token_count, route_count = route_ids.shape
    entries = token_count * route_count
    flat_ids = route_ids.reshape(entries)
    order = jnp.arange(entries, dtype=jnp.int32)
    earlier = (order[None, :] < order[:, None]) & (flat_ids[None, :] == flat_ids[:, None])
    slot_of = jnp.sum(earlier.astype(jnp.int32), axis=1)
    slot_table = jnp.full((capacity, node_count), entries, jnp.int32)
    slot_table = slot_table.at[slot_of, flat_ids].set(order, mode="drop")
    return (slot_of, flat_ids, slot_table)


def general_body(layer_input, out_grad, routes, gates, gate_weight, up_weight, down_weight):
    node_count = lax.axis_size("node")
    local_count = lax.axis_size("local")
    token_count = layer_input.shape[1]
    quarter = layer_input.shape[2]
    route_count = routes.shape[2]
    capacity = min(2 * token_count * route_count // node_count, 3 * token_count // 4)
    entries = token_count * route_count
    slot_of, flat_ids, slot_table = slot_tables(routes[0], node_count, capacity)
    live_slots = slot_table < entries
    entry_idx = jnp.minimum(slot_table, entries - 1)
    token_idx = entry_idx // route_count
    live_scale = live_slots.astype(BF16)
    send_input = layer_input[0][token_idx] * live_scale[:, :, None]
    send_grads = out_grad[0][token_idx] * live_scale[:, :, None]
    send_gates = gates[0].reshape(entries)[entry_idx] * live_scale
    wide_shape = (capacity, node_count, local_count, quarter)

    def exchange(value):
        return lax.all_to_all(value, ("node", "local"), split_axis=1, concat_axis=1, tiled=True)

    def widen(value):
        wide = jnp.broadcast_to(value[:, :, None, :], wide_shape)
        return wide.reshape(capacity, node_count * local_count, quarter)

    wide_gates = jnp.broadcast_to(send_gates[:, :, None], wide_shape[:3])
    got_input = exchange(widen(send_input))
    got_grads = exchange(widen(send_grads))
    got_gates = exchange(wide_gates.reshape(capacity, node_count * local_count))
    row_total = capacity * node_count
    flat_input = got_input.reshape(row_total, -1)
    flat_grads = got_grads.reshape(row_total, -1)
    own_column = (jnp.arange(local_count, dtype=jnp.int32) == lax.axis_index("local")).astype(F32)
    gate_column = jnp.sum(
        got_gates.reshape(capacity, node_count, local_count).astype(F32) * own_column, axis=2
    ).reshape(row_total, 1)
    w_gate = gate_weight[0, 0]
    w_up = up_weight[0, 0]
    w_down = down_weight[0, 0]
    pre_gate = jnp.dot(flat_input, w_gate, preferred_element_type=F32)
    pre_up = jnp.dot(flat_input, w_up, preferred_element_type=F32)
    hidden_raw = jnp.dot(flat_grads, w_down.T, preferred_element_type=F32)
    gate_part, gated_act, grad_gate, grad_up = unit_math(pre_gate, pre_up, hidden_raw, gate_column)
    unit_terms = jnp.dot(grad_gate, w_gate.T, preferred_element_type=F32)
    unit_terms = unit_terms + jnp.dot(grad_up, w_up.T, preferred_element_type=F32)
    gate_spread = jnp.broadcast_to(gate_part.reshape(capacity, node_count, 1), wide_shape[:3])
    got_rows = exchange(unit_terms.astype(BF16).reshape(capacity, node_count * local_count, quarter))
    got_gate = exchange(gate_spread.astype(BF16).reshape(capacity, node_count * local_count))
    route_rows = jnp.sum(got_rows.reshape(wide_shape), axis=2, dtype=F32)
    route_rows = lax.optimization_barrier(route_rows.astype(BF16))
    route_gate = jnp.sum(got_gate.reshape(wide_shape[:3]), axis=2, dtype=F32)
    route_gate = lax.optimization_barrier(route_gate.astype(BF16))
    flat_rows = route_rows.reshape(row_total, quarter)
    position = jnp.minimum(slot_of * node_count + flat_ids, row_total - 1)
    per_entry = flat_rows[position].reshape(token_count, route_count, quarter)
    input_grad = jnp.sum(per_entry, axis=1, dtype=F32).astype(BF16)
    gate_grad = (
        route_gate.reshape(row_total)[position].astype(F32).reshape(1, token_count, route_count)
    )
    passed = from_behind(input_grad[None], "section", -1)
    gate_wgrad = jnp.dot(flat_input.T, grad_gate, preferred_element_type=F32).astype(BF16)
    up_wgrad = jnp.dot(flat_input.T, grad_up, preferred_element_type=F32).astype(BF16)
    down_wgrad = jnp.dot(gated_act.T, flat_grads, preferred_element_type=F32).astype(BF16)
    return (passed, gate_grad, gate_wgrad[None, None], up_wgrad[None, None], down_wgrad[None, None])


def unit_math(pre_gate, pre_up, hidden_raw, gate_column):
    sigmoid_gate = jax.nn.sigmoid(pre_gate)
    swish_gate = pre_gate * sigmoid_gate
    activation = swish_gate * pre_up
    gate_part = jnp.sum(activation * hidden_raw, axis=1, keepdims=True)
    gated_act = (gate_column * activation).astype(BF16)
    scaled = gate_column * hidden_raw
    grad_gate = (scaled * pre_up * sigmoid_gate * (1.0 + pre_gate * (1.0 - sigmoid_gate))).astype(
        BF16
    )
    grad_up = (scaled * swish_gate).astype(BF16)
    return gate_part, gated_act, grad_gate, grad_up


def layer_kernel(
    T, K, C, F,
    x_hbm, dy_hbm, routes_ref, gates_ref, wg_hbm, wu_hbm, wd_hbm,
    ig_ref, gate_out_ref, gw_ref, uw_ref, dw_ref,
    pick, xf, dyv, rx, rd, xs, dys, gsend, grecv, pg, pu, hr, gg_ref, gu_ref, ga_ref,
    sa, ra, sb, rb, own, sc, rc, fz, zr, gts, gtr,
    send_sem, recv_sem, load_sem,
):
    n = lax.axis_index("node")
    l = lax.axis_index("local")
    xi = l // 2
    ci = l % 2
    q_me = l
    q_xm = 2 * (1 - xi) + ci
    q_cm = 2 * xi + 1 - ci
    q_cx = 2 * (1 - xi) + 1 - ci
    x_mate = {"local": q_xm}
    c_mate = {"local": q_cm}
    y_mate = {"node": 1 - n}

    z = lax.axis_index("section")
    z_count = lax.axis_size("section")
    x_load = pltpu.make_async_copy(x_hbm, xf.at[q_me], load_sem.at[3])
    dy_load = pltpu.make_async_copy(dy_hbm, dyv, load_sem.at[4])
    dy_load.start()
    x_load.start()
    loads = [
        pltpu.make_async_copy(wg_hbm, gw_ref, load_sem.at[0]),
        pltpu.make_async_copy(wu_hbm, uw_ref, load_sem.at[1]),
        pltpu.make_async_copy(wd_hbm, dw_ref, load_sem.at[2]),
    ]

    barrier = pltpu.get_barrier_semaphore()
    for dn in range(2):
        for dl in range(4):
            if dn or dl:
                pl.semaphore_signal(
                    barrier, inc=1, device_id_type=MESH,
                    device_id={"node": lax.rem(n + dn, 2), "local": lax.rem(l + dl, 4)},
                )
    for dz in (1, z_count - 1):
        pl.semaphore_signal(
            barrier, inc=1, device_id_type=MESH, device_id={"section": lax.rem(z + dz, z_count)}
        )
    pl.semaphore_wait(barrier, 9)

    sent = []

    def send(i, src, dst, dev):
        d = pltpu.make_async_remote_copy(
            src_ref=src, dst_ref=dst, send_sem=send_sem.at[i], recv_sem=recv_sem.at[i],
            device_id=dev, device_id_type=MESH,
        )
        d.start()
        sent.append(d)
        return d

    m0 = send(0, x_hbm, xf.at[q_me], x_mate)

    ids = routes_ref[...]
    before = lax.broadcasted_iota(jnp.int32, (T, T), 0) < lax.broadcasted_iota(jnp.int32, (T, T), 1)
    before = jnp.where(before, 1.0, 0.0).astype(BF16)
    slot = lax.broadcasted_iota(jnp.int32, (K, T), 0).astype(F32)
    gate_row = gates_ref[...].astype(F32)
    columns = []
    for g in range(2):
        named = jnp.where(ids == (n if g == 0 else 1 - n), 1.0, 0.0)
        rank = jnp.dot(
            jnp.broadcast_to(named, (16, T)).astype(BF16), before, preferred_element_type=F32
        )[0:1]
        hit = jnp.where(rank == slot, jnp.broadcast_to(named, (K, T)), 0.0)
        pick[g] = hit.astype(BF16)
        columns.append(jnp.sum(hit * gate_row, axis=1, keepdims=True))

    def select(g, rows):
        return jnp.dot(pick[g], rows, preferred_element_type=F32).astype(BF16)

    dy_load.wait()
    dys[...] = select(1, dyv[...])
    m3 = send(3, dys, rd.at[q_me, 1], y_mate)
    gsend[...] = jnp.broadcast_to(columns[1], (K, 128)).astype(BF16)
    m14 = send(14, gsend, grecv, y_mate)
    rd[q_me, 0] = select(0, dyv[...])
    m4 = send(4, rd.at[q_me, 0], rd.at[q_me, 0], x_mate)
    x_load.wait()
    xs[0] = select(1, xf[q_me])
    m10 = send(10, xs.at[0], rx.at[q_me, 1], y_mate)
    m5 = send(5, rd.at[q_me, 0], rd.at[q_me, 0], c_mate)
    m1 = send(1, xf.at[q_me], xf.at[q_me], c_mate)
    for d in loads:
        d.start()
    rx[q_me, 0] = select(0, xf[q_me])

    m0.wait_recv()
    xs[1] = select(1, xf[q_xm])
    m11 = send(11, xs.at[1], rx.at[q_xm, 1], y_mate)
    m2 = send(2, xf.at[q_xm], xf.at[q_xm], c_mate)
    m3.wait_recv()
    m7 = send(7, rd.at[q_me, 1], rd.at[q_me, 1], x_mate)
    m8 = send(8, rd.at[q_me, 1], rd.at[q_me, 1], c_mate)
    rx[q_xm, 0] = select(0, xf[q_xm])
    m1.wait_recv()
    rx[q_cm, 0] = select(0, xf[q_cm])
    m4.wait_recv()
    m6 = send(6, rd.at[q_xm, 0], rd.at[q_xm, 0], c_mate)
    m10.wait_recv()
    m12 = send(12, rx.at[q_me, 1], rx.at[q_me, 1], c_mate)
    m2.wait_recv()
    rx[q_cx, 0] = select(0, xf[q_cx])

    for d in loads:
        d.wait()
    pg[...] = jnp.zeros_like(pg)
    pu[...] = jnp.zeros_like(pu)
    hr[...] = jnp.zeros_like(hr)

    def project(q):
        rows = rx[q].reshape(2 * K, C)
        pg[...] += jnp.dot(rows, gw_ref[q], preferred_element_type=F32)
        pu[...] += jnp.dot(rows, uw_ref[q], preferred_element_type=F32)

    def hidden(q):
        rows = rd[q].reshape(2 * K, C)
        wide = pl.ds(pl.multiple_of(q * C, 256), C)
        hr[...] += lax.dot_general(rows, dw_ref[:, wide], NT, preferred_element_type=F32)

    project(q_me)
    m12.wait_recv()
    project(q_cm)
    m5.wait_recv()
    m8.wait_recv()
    m6.wait_recv()
    hidden(q_me)
    hidden(q_cm)
    m7.wait_recv()
    m9 = send(9, rd.at[q_xm, 1], rd.at[q_xm, 1], c_mate)
    m11.wait_recv()
    m13 = send(13, rx.at[q_xm, 1], rx.at[q_xm, 1], c_mate)
    hidden(q_xm)
    project(q_xm)
    m9.wait_recv()
    hidden(q_cx)
    m13.wait_recv()
    project(q_cx)
    m14.wait_recv()

    parts = []
    for g in range(2):
        rows = pl.ds(g * K, K)
        column = columns[0] if g == 0 else grecv[:, 0:1].astype(F32)
        part, act, d_gate, d_up = unit_math(pg[rows], pu[rows], hr[rows], column)
        ga_ref[rows] = act
        gg_ref[rows] = d_gate
        gu_ref[rows] = d_up
        parts.append(part)

    def terms(q, j):
        at = pl.ds(j * 256, 256)
        t = lax.dot_general(gg_ref[...], gw_ref[q, at], NT, preferred_element_type=F32)
        t += lax.dot_general(gu_ref[...], uw_ref[q, at], NT, preferred_element_type=F32)
        return t.astype(BF16).reshape(2, K, 256)

    chunks = C // 256
    a0, a1, b, c, last = [], [], [], [], []

    def across(j):
        a0[j].wait_recv()
        sb[j] = (sb[j].astype(F32) + ra[0, j].astype(F32)).astype(BF16)
        b.append(send(15 + 2 * chunks + j, sb.at[j], rb.at[j], x_mate))

    for j in range(chunks):
        sa[0, j] = terms(q_cx, j)
        a0.append(send(15 + j, sa.at[0, j], ra.at[0, j], c_mate))
        sb[j] = terms(q_xm, j)
        if j:
            across(j - 1)
    across(chunks - 1)

    eye = lax.broadcasted_iota(jnp.int32, (K, K), 0) == lax.broadcasted_iota(jnp.int32, (K, K), 1)
    for g in range(2):
        part = parts[g].astype(BF16).astype(F32)
        row = jnp.sum(jnp.where(eye, part, 0.0), axis=0, keepdims=True)
        gts[g] = jnp.broadcast_to(row, (16, K)).astype(BF16)
    gtr[l] = gts[0]
    gate_sent = []
    first = 15 + 5 * chunks
    for k in range(1, 4):
        gate_sent.append(
            send(first + k - 1, gts.at[0], gtr.at[l], {"local": lax.rem(l + k, 4)})
        )
    for k in range(4):
        gate_sent.append(
            send(
                first + 3 + k, gts.at[1], gtr.at[4 + l],
                {"node": 1 - n, "local": lax.rem(l + k, 4)},
            )
        )

    for j in range(chunks):
        sa[1, j] = terms(q_cm, j)
        a1.append(send(15 + chunks + j, sa.at[1, j], ra.at[1, j], c_mate))
        own[j] = terms(q_me, j)

    def weights(j):
        @pl.loop(0, 4)
        def _(q):
            at = pl.ds(j * 256, 256)
            rows = rx[q, :, :, at].reshape(2 * K, 256)
            grads = rd[q, :, :, at].reshape(2 * K, 256)
            gw_ref[q, at] = lax.dot_general(
                rows, gg_ref[...], TN, preferred_element_type=F32
            ).astype(BF16)
            uw_ref[q, at] = lax.dot_general(
                rows, gu_ref[...], TN, preferred_element_type=F32
            ).astype(BF16)
            wide = pl.ds(pl.multiple_of(q * C + j * 256, 256), 256)
            dw_ref[:, wide] = lax.dot_general(
                ga_ref[...], grads, TN, preferred_element_type=F32
            ).astype(BF16)

    def finish(j):
        c[j].wait_recv()
        t = lax.dot_general(pick[0], own[j, 0], TN, preferred_element_type=F32)
        t += lax.dot_general(pick[1], rc[j], TN, preferred_element_type=F32)
        fz[j] = t.astype(BF16)
        last.append(
            send(
                15 + 4 * chunks + j, fz.at[j], zr.at[j],
                {"section": lax.rem(z + z_count - 1, z_count)},
            )
        )

    for j in range(chunks):
        a1[j].wait_recv()
        b[j].wait_recv()
        whole = own[j].astype(F32) + ra[1, j].astype(F32) + rb[j].astype(F32)
        whole = whole.astype(BF16)
        sc[j] = whole[1]
        c.append(send(15 + 3 * chunks + j, sc.at[j], rc.at[j], y_mate))
        own[j, 0] = whole[0]
        if j:
            finish(j - 1)
        weights(j)
    for d in gate_sent:
        d.wait_recv()
    total = jnp.zeros((16, T), F32)
    for g in range(2):
        row = gtr[4 * g].astype(F32)
        for k in range(1, 4):
            row += gtr[4 * g + k].astype(F32)
        total += jnp.dot(row.astype(BF16), pick[g], preferred_element_type=F32)
    gate_out_ref[...] = total[0:1]
    finish(chunks - 1)
    for j in range(chunks):
        last[j].wait_recv()
        ig_ref[:, j * 256 : (j + 1) * 256] = zr[j]
    for d in sent:
        d.wait_send()


def store_kernel(gw_ref, uw_ref, dw_ref, gw_out, uw_out, dw_out, sem):
    copies = []
    for k, (src, dst) in enumerate(((gw_ref, gw_out), (uw_ref, uw_out), (dw_ref, dw_out))):
        part = src.shape[0] // 4
        for i in range(4):
            at = pl.ds(i * part, part)
            copies.append(pltpu.make_async_copy(src.at[at], dst.at[at], sem.at[4 * k + i]))
    for d in copies:
        d.start()
    for d in copies:
        d.wait()


def fused_body(layer_input, out_grad, routes, gates, gate_weight, up_weight, down_weight):
    T, C = layer_input.shape[1:]
    D, F = gate_weight.shape[2:]
    K = -(-(3 * T // 4) // 128) * 128
    vmem = pl.BlockSpec(memory_space=pltpu.VMEM)
    hbm = pl.BlockSpec(memory_space=pl.ANY)
    shape = jax.ShapeDtypeStruct
    rows = (4, 2, K, C)
    chunk = (C // 256, K, 256)
    pair = (C // 256, 2, K, 256)
    last = (C // 256, T, 256)
    ig, gate_grad, gw, uw, dw = pl.pallas_call(
        functools.partial(layer_kernel, T, K, C, F),
        out_shape=(
            shape((T, C), BF16), shape((1, T), F32),
            shape((4, C, F), BF16), shape((4, C, F), BF16), shape((F, D), BF16),
        ),
        in_specs=[hbm] * 2 + [vmem] * 2 + [hbm] * 3,
        out_specs=(vmem,) * 5,
        scratch_shapes=[
            pltpu.VMEM((2, K, T), BF16), pltpu.VMEM((4, T, C), BF16), pltpu.VMEM((T, C), BF16),
            pltpu.VMEM(rows, BF16), pltpu.VMEM(rows, BF16),
            pltpu.VMEM((2, K, C), BF16), pltpu.VMEM((K, C), BF16),
            pltpu.VMEM((K, 128), BF16), pltpu.VMEM((K, 128), BF16),
            pltpu.VMEM((2 * K, F), F32), pltpu.VMEM((2 * K, F), F32), pltpu.VMEM((2 * K, F), F32),
            pltpu.VMEM((2 * K, F), BF16), pltpu.VMEM((2 * K, F), BF16), pltpu.VMEM((2 * K, F), BF16),
            pltpu.VMEM((2,) + pair, BF16), pltpu.VMEM((2,) + pair, BF16),
            pltpu.VMEM(pair, BF16), pltpu.VMEM(pair, BF16), pltpu.VMEM(pair, BF16),
            pltpu.VMEM(chunk, BF16), pltpu.VMEM(chunk, BF16),
            pltpu.VMEM(last, BF16), pltpu.VMEM(last, BF16),
            pltpu.VMEM((2, 16, K), BF16), pltpu.VMEM((8, 16, K), BF16),
            pltpu.SemaphoreType.DMA((22 + 5 * (C // 256),)),
            pltpu.SemaphoreType.DMA((22 + 5 * (C // 256),)),
            pltpu.SemaphoreType.DMA((5,)),
        ],
        compiler_params=pltpu.CompilerParams(
            collective_id=0, has_side_effects=True, vmem_limit_bytes=41 * 2**20
        ),
        name="layer",
    )(
        layer_input[0], out_grad[0], routes.reshape(1, T), gates.reshape(1, T),
        gate_weight.reshape(4, C, F), up_weight.reshape(4, C, F), down_weight.reshape(F, D),
    )
    gw, uw, dw = pl.pallas_call(
        store_kernel,
        out_shape=(shape((D, F), BF16), shape((D, F), BF16), shape((F, D), BF16)),
        in_specs=[vmem] * 3,
        out_specs=(hbm,) * 3,
        scratch_shapes=[pltpu.SemaphoreType.DMA((12,))],
        compiler_params=pltpu.CompilerParams(vmem_limit_bytes=16 * 2**20),
        name="store",
    )(gw.reshape(D, F), uw.reshape(D, F), dw)
    return (
        ig[None], gate_grad.reshape(1, T, 1), gw[None, None], uw[None, None], dw[None, None]
    )


def body(*args):
    routes, gate_weight = args[2], args[4]
    small = lax.axis_size("node") == 2 and lax.axis_size("local") == 4
    if small and routes.shape[2] == 1 and gate_weight.shape[1] == 1:
        return fused_body(*args)
    return general_body(*args)


def solution(mesh):
    return jax.shard_map(
        body,
        mesh=mesh,
        in_specs=(
            P("section", "node", "local"),
            P("section", "node", "local"),
            P("section", "node", None),
            P("section", "node", None),
            P("section", "node", None, "local"),
            P("section", "node", None, "local"),
            P("section", "node", "local", None),
        ),
        out_specs=(
            P("section", "node", "local"),
            P("section", "node", None),
            P("section", "node", None, "local"),
            P("section", "node", None, "local"),
            P("section", "node", "local", None),
        ),
        check_vma=False,
    )
```

```python
import functools

import jax
import jax.numpy as jnp
from jax import lax
from jax.experimental import pallas as pl
from jax.experimental.pallas import tpu as pltpu
from jax.sharding import PartitionSpec as P

F32 = jnp.float32
BF16 = jnp.bfloat16
MESH = pl.DeviceIdType.MESH
NT = (((1,), (1,)), ((), ()))
TN = (((0,), (0,)), ((), ()))


def from_behind(value, axis, by):
    length = lax.axis_size(axis)
    return lax.ppermute(value, axis, [(i, (i + by) % length) for i in range(length)])


def slot_tables(route_ids, node_count, capacity):
    token_count, route_count = route_ids.shape
    entries = token_count * route_count
    flat_ids = route_ids.reshape(entries)
    order = jnp.arange(entries, dtype=jnp.int32)
    earlier = (order[None, :] < order[:, None]) & (flat_ids[None, :] == flat_ids[:, None])
    slot_of = jnp.sum(earlier.astype(jnp.int32), axis=1)
    slot_table = jnp.full((capacity, node_count), entries, jnp.int32)
    slot_table = slot_table.at[slot_of, flat_ids].set(order, mode="drop")
    return (slot_of, flat_ids, slot_table)


def general_body(layer_input, out_grad, routes, gates, gate_weight, up_weight, down_weight):
    node_count = lax.axis_size("node")
    local_count = lax.axis_size("local")
    token_count = layer_input.shape[1]
    quarter = layer_input.shape[2]
    route_count = routes.shape[2]
    capacity = min(2 * token_count * route_count // node_count, 3 * token_count // 4)
    entries = token_count * route_count
    slot_of, flat_ids, slot_table = slot_tables(routes[0], node_count, capacity)
    live_slots = slot_table < entries
    entry_idx = jnp.minimum(slot_table, entries - 1)
    token_idx = entry_idx // route_count
    live_scale = live_slots.astype(BF16)
    send_input = layer_input[0][token_idx] * live_scale[:, :, None]
    send_grads = out_grad[0][token_idx] * live_scale[:, :, None]
    send_gates = gates[0].reshape(entries)[entry_idx] * live_scale
    wide_shape = (capacity, node_count, local_count, quarter)

    def exchange(value):
        return lax.all_to_all(value, ("node", "local"), split_axis=1, concat_axis=1, tiled=True)

    def widen(value):
        wide = jnp.broadcast_to(value[:, :, None, :], wide_shape)
        return wide.reshape(capacity, node_count * local_count, quarter)

    wide_gates = jnp.broadcast_to(send_gates[:, :, None], wide_shape[:3])
    got_input = exchange(widen(send_input))
    got_grads = exchange(widen(send_grads))
    got_gates = exchange(wide_gates.reshape(capacity, node_count * local_count))
    row_total = capacity * node_count
    flat_input = got_input.reshape(row_total, -1)
    flat_grads = got_grads.reshape(row_total, -1)
    own_column = (jnp.arange(local_count, dtype=jnp.int32) == lax.axis_index("local")).astype(F32)
    gate_column = jnp.sum(
        got_gates.reshape(capacity, node_count, local_count).astype(F32) * own_column, axis=2
    ).reshape(row_total, 1)
    w_gate = gate_weight[0, 0]
    w_up = up_weight[0, 0]
    w_down = down_weight[0, 0]
    pre_gate = jnp.dot(flat_input, w_gate, preferred_element_type=F32)
    pre_up = jnp.dot(flat_input, w_up, preferred_element_type=F32)
    hidden_raw = jnp.dot(flat_grads, w_down.T, preferred_element_type=F32)
    gate_part, gated_act, grad_gate, grad_up = unit_math(pre_gate, pre_up, hidden_raw, gate_column)
    unit_terms = jnp.dot(grad_gate, w_gate.T, preferred_element_type=F32)
    unit_terms = unit_terms + jnp.dot(grad_up, w_up.T, preferred_element_type=F32)
    gate_spread = jnp.broadcast_to(gate_part.reshape(capacity, node_count, 1), wide_shape[:3])
    got_rows = exchange(unit_terms.astype(BF16).reshape(capacity, node_count * local_count, quarter))
    got_gate = exchange(gate_spread.astype(BF16).reshape(capacity, node_count * local_count))
    route_rows = jnp.sum(got_rows.reshape(wide_shape), axis=2, dtype=F32)
    route_rows = lax.optimization_barrier(route_rows.astype(BF16))
    route_gate = jnp.sum(got_gate.reshape(wide_shape[:3]), axis=2, dtype=F32)
    route_gate = lax.optimization_barrier(route_gate.astype(BF16))
    flat_rows = route_rows.reshape(row_total, quarter)
    position = jnp.minimum(slot_of * node_count + flat_ids, row_total - 1)
    per_entry = flat_rows[position].reshape(token_count, route_count, quarter)
    input_grad = jnp.sum(per_entry, axis=1, dtype=F32).astype(BF16)
    gate_grad = (
        route_gate.reshape(row_total)[position].astype(F32).reshape(1, token_count, route_count)
    )
    passed = from_behind(input_grad[None], "section", -1)
    gate_wgrad = jnp.dot(flat_input.T, grad_gate, preferred_element_type=F32).astype(BF16)
    up_wgrad = jnp.dot(flat_input.T, grad_up, preferred_element_type=F32).astype(BF16)
    down_wgrad = jnp.dot(gated_act.T, flat_grads, preferred_element_type=F32).astype(BF16)
    return (passed, gate_grad, gate_wgrad[None, None], up_wgrad[None, None], down_wgrad[None, None])


def unit_math(pre_gate, pre_up, hidden_raw, gate_column):
    sigmoid_gate = jax.nn.sigmoid(pre_gate)
    swish_gate = pre_gate * sigmoid_gate
    activation = swish_gate * pre_up
    gate_part = jnp.sum(activation * hidden_raw, axis=1, keepdims=True)
    gated_act = (gate_column * activation).astype(BF16)
    scaled = gate_column * hidden_raw
    grad_gate = (scaled * pre_up * sigmoid_gate * (1.0 + pre_gate * (1.0 - sigmoid_gate))).astype(
        BF16
    )
    grad_up = (scaled * swish_gate).astype(BF16)
    return gate_part, gated_act, grad_gate, grad_up


def layer_kernel(
    T, K, C, F,
    x_hbm, dy_hbm, routes_hbm, gates_ref, wg_hbm, wu_hbm, wd_hbm,
    ig_ref, gate_out_ref, gw_ref, uw_ref, dw_ref,
    routes_ref, pick, xf, dyv, rx, rd, xs, dys, gsend, grecv, pg, pu, hr, gg_ref, gu_ref, ga_ref,
    sa, ra, sb, rb, own, sc, rc, fz, zr, gts, gtr,
    send_sem, recv_sem, load_sem,
):
    n = lax.axis_index("node")
    l = lax.axis_index("local")
    xi = l // 2
    ci = l % 2
    q_me = l
    q_xm = 2 * (1 - xi) + ci
    q_cm = 2 * xi + 1 - ci
    q_cx = 2 * (1 - xi) + 1 - ci
    x_mate = {"local": q_xm}
    c_mate = {"local": q_cm}
    y_mate = {"node": 1 - n}

    z = lax.axis_index("section")
    z_count = lax.axis_size("section")
    x_load = pltpu.make_async_copy(x_hbm, xf.at[q_me], load_sem.at[3])
    dy_load = pltpu.make_async_copy(dy_hbm, dyv, load_sem.at[4])
    routes_load = pltpu.make_async_copy(routes_hbm, routes_ref, load_sem.at[5])
    routes_load.start()
    dy_load.start()
    x_load.start()
    loads = [
        pltpu.make_async_copy(wg_hbm, gw_ref, load_sem.at[0]),
        pltpu.make_async_copy(wu_hbm, uw_ref, load_sem.at[1]),
        pltpu.make_async_copy(wd_hbm, dw_ref, load_sem.at[2]),
    ]

    barrier = pltpu.get_barrier_semaphore()
    for dn in range(2):
        for dl in range(4):
            if dn or dl:
                pl.semaphore_signal(
                    barrier, inc=1, device_id_type=MESH,
                    device_id={"node": lax.rem(n + dn, 2), "local": lax.rem(l + dl, 4)},
                )
    for dz in (1, z_count - 1):
        pl.semaphore_signal(
            barrier, inc=1, device_id_type=MESH, device_id={"section": lax.rem(z + dz, z_count)}
        )
    pl.semaphore_wait(barrier, 9)

    sent = []

    def send(i, src, dst, dev):
        d = pltpu.make_async_remote_copy(
            src_ref=src, dst_ref=dst, send_sem=send_sem.at[i], recv_sem=recv_sem.at[i],
            device_id=dev, device_id_type=MESH,
        )
        d.start()
        sent.append(d)
        return d

    m0 = send(0, x_hbm, xf.at[q_me], x_mate)

    routes_load.wait()
    ids = routes_ref[...]
    before = lax.broadcasted_iota(jnp.int32, (T, T), 0) < lax.broadcasted_iota(jnp.int32, (T, T), 1)
    before = jnp.where(before, 1.0, 0.0).astype(BF16)
    slot = lax.broadcasted_iota(jnp.int32, (K, T), 0).astype(F32)
    gate_row = gates_ref[...].astype(F32)
    columns = []
    for g in range(2):
        named = jnp.where(ids == (n if g == 0 else 1 - n), 1.0, 0.0)
        rank = jnp.dot(
            jnp.broadcast_to(named, (16, T)).astype(BF16), before, preferred_element_type=F32
        )[0:1]
        hit = jnp.where(rank == slot, jnp.broadcast_to(named, (K, T)), 0.0)
        pick[g] = hit.astype(BF16)
        columns.append(jnp.sum(hit * gate_row, axis=1, keepdims=True))

    def select(g, rows):
        return jnp.dot(pick[g], rows, preferred_element_type=F32).astype(BF16)

    dy_load.wait()
    dys[...] = select(1, dyv[...])
    m3 = send(3, dys, rd.at[q_me, 1], y_mate)
    gsend[...] = jnp.broadcast_to(columns[1], (K, 128)).astype(BF16)
    m14 = send(14, gsend, grecv, y_mate)
    rd[q_me, 0] = select(0, dyv[...])
    m4 = send(4, rd.at[q_me, 0], rd.at[q_me, 0], x_mate)
    x_load.wait()
    xs[0] = select(1, xf[q_me])
    m10 = send(10, xs.at[0], rx.at[q_me, 1], y_mate)
    m5 = send(5, rd.at[q_me, 0], rd.at[q_me, 0], c_mate)
    m1 = send(1, xf.at[q_me], xf.at[q_me], c_mate)
    for d in loads:
        d.start()
    rx[q_me, 0] = select(0, xf[q_me])

    m0.wait_recv()
    xs[1] = select(1, xf[q_xm])
    m11 = send(11, xs.at[1], rx.at[q_xm, 1], y_mate)
    m2 = send(2, xf.at[q_xm], xf.at[q_xm], c_mate)
    m3.wait_recv()
    m7 = send(7, rd.at[q_me, 1], rd.at[q_me, 1], x_mate)
    m8 = send(8, rd.at[q_me, 1], rd.at[q_me, 1], c_mate)
    rx[q_xm, 0] = select(0, xf[q_xm])
    m1.wait_recv()
    rx[q_cm, 0] = select(0, xf[q_cm])
    m4.wait_recv()
    m6 = send(6, rd.at[q_xm, 0], rd.at[q_xm, 0], c_mate)
    m10.wait_recv()
    m12 = send(12, rx.at[q_me, 1], rx.at[q_me, 1], c_mate)
    m2.wait_recv()
    rx[q_cx, 0] = select(0, xf[q_cx])

    for d in loads:
        d.wait()
    pg[...] = jnp.zeros_like(pg)
    pu[...] = jnp.zeros_like(pu)
    hr[...] = jnp.zeros_like(hr)

    def project(q):
        rows = rx[q].reshape(2 * K, C)
        pg[...] += jnp.dot(rows, gw_ref[q], preferred_element_type=F32)
        pu[...] += jnp.dot(rows, uw_ref[q], preferred_element_type=F32)

    def hidden(q):
        rows = rd[q].reshape(2 * K, C)
        wide = pl.ds(pl.multiple_of(q * C, 256), C)
        hr[...] += lax.dot_general(rows, dw_ref[:, wide], NT, preferred_element_type=F32)

    project(q_me)
    m12.wait_recv()
    project(q_cm)
    m5.wait_recv()
    m8.wait_recv()
    m6.wait_recv()
    hidden(q_me)
    hidden(q_cm)
    m7.wait_recv()
    m9 = send(9, rd.at[q_xm, 1], rd.at[q_xm, 1], c_mate)
    m11.wait_recv()
    m13 = send(13, rx.at[q_xm, 1], rx.at[q_xm, 1], c_mate)
    hidden(q_xm)
    project(q_xm)
    m9.wait_recv()
    hidden(q_cx)
    m13.wait_recv()
    project(q_cx)
    m14.wait_recv()

    parts = []
    for g in range(2):
        rows = pl.ds(g * K, K)
        column = columns[0] if g == 0 else grecv[:, 0:1].astype(F32)
        part, act, d_gate, d_up = unit_math(pg[rows], pu[rows], hr[rows], column)
        ga_ref[rows] = act
        gg_ref[rows] = d_gate
        gu_ref[rows] = d_up
        parts.append(part)

    def terms(q, j):
        at = pl.ds(j * 256, 256)
        t = lax.dot_general(gg_ref[...], gw_ref[q, at], NT, preferred_element_type=F32)
        t += lax.dot_general(gu_ref[...], uw_ref[q, at], NT, preferred_element_type=F32)
        return t.astype(BF16).reshape(2, K, 256)

    chunks = C // 256
    a0, a1, b, c, last = [], [], [], [], []

    def across(j):
        a0[j].wait_recv()
        sb[j] = (sb[j].astype(F32) + ra[0, j].astype(F32)).astype(BF16)
        b.append(send(15 + 2 * chunks + j, sb.at[j], rb.at[j], x_mate))

    for j in range(chunks):
        sa[0, j] = terms(q_cx, j)
        a0.append(send(15 + j, sa.at[0, j], ra.at[0, j], c_mate))
        sb[j] = terms(q_xm, j)
        if j:
            across(j - 1)
    across(chunks - 1)

    eye = lax.broadcasted_iota(jnp.int32, (K, K), 0) == lax.broadcasted_iota(jnp.int32, (K, K), 1)
    for g in range(2):
        part = parts[g].astype(BF16).astype(F32)
        row = jnp.sum(jnp.where(eye, part, 0.0), axis=0, keepdims=True)
        gts[g] = jnp.broadcast_to(row, (16, K)).astype(BF16)
    gtr[l] = gts[0]
    gate_sent = []
    first = 15 + 5 * chunks
    for k in range(1, 4):
        gate_sent.append(
            send(first + k - 1, gts.at[0], gtr.at[l], {"local": lax.rem(l + k, 4)})
        )
    for k in range(4):
        gate_sent.append(
            send(
                first + 3 + k, gts.at[1], gtr.at[4 + l],
                {"node": 1 - n, "local": lax.rem(l + k, 4)},
            )
        )

    for j in range(chunks):
        sa[1, j] = terms(q_cm, j)
        a1.append(send(15 + chunks + j, sa.at[1, j], ra.at[1, j], c_mate))
        own[j] = terms(q_me, j)

    def weights(j):
        @pl.loop(0, 4)
        def _(q):
            at = pl.ds(j * 256, 256)
            rows = rx[q, :, :, at].reshape(2 * K, 256)
            grads = rd[q, :, :, at].reshape(2 * K, 256)
            gw_ref[q, at] = lax.dot_general(
                rows, gg_ref[...], TN, preferred_element_type=F32
            ).astype(BF16)
            uw_ref[q, at] = lax.dot_general(
                rows, gu_ref[...], TN, preferred_element_type=F32
            ).astype(BF16)
            wide = pl.ds(pl.multiple_of(q * C + j * 256, 256), 256)
            dw_ref[:, wide] = lax.dot_general(
                ga_ref[...], grads, TN, preferred_element_type=F32
            ).astype(BF16)

    def finish(j):
        c[j].wait_recv()
        t = lax.dot_general(pick[0], own[j, 0], TN, preferred_element_type=F32)
        t += lax.dot_general(pick[1], rc[j], TN, preferred_element_type=F32)
        fz[j] = t.astype(BF16)
        last.append(
            send(
                15 + 4 * chunks + j, fz.at[j], zr.at[j],
                {"section": lax.rem(z + z_count - 1, z_count)},
            )
        )

    for j in range(chunks):
        a1[j].wait_recv()
        b[j].wait_recv()
        whole = own[j].astype(F32) + ra[1, j].astype(F32) + rb[j].astype(F32)
        whole = whole.astype(BF16)
        sc[j] = whole[1]
        c.append(send(15 + 3 * chunks + j, sc.at[j], rc.at[j], y_mate))
        own[j, 0] = whole[0]
        if j:
            finish(j - 1)
        weights(j)
    for d in gate_sent:
        d.wait_recv()
    total = jnp.zeros((16, T), F32)
    for g in range(2):
        row = gtr[4 * g].astype(F32)
        for k in range(1, 4):
            row += gtr[4 * g + k].astype(F32)
        total += jnp.dot(row.astype(BF16), pick[g], preferred_element_type=F32)
    gate_out_ref[...] = total[0:1]
    finish(chunks - 1)
    for j in range(chunks):
        last[j].wait_recv()
        ig_ref[:, j * 256 : (j + 1) * 256] = zr[j]
    for d in sent:
        d.wait_send()


def store_kernel(ig_ref, gate_ref, gw_ref, uw_ref, dw_ref, ig_out, gate_out, gw_out, uw_out, dw_out, sem):
    copies = []
    for k, (src, dst) in enumerate(((gw_ref, gw_out), (uw_ref, uw_out), (dw_ref, dw_out))):
        part = src.shape[0] // 4
        for i in range(4):
            at = pl.ds(i * part, part)
            copies.append(pltpu.make_async_copy(src.at[at], dst.at[at], sem.at[4 * k + i]))
    copies.append(pltpu.make_async_copy(ig_ref, ig_out, sem.at[12]))
    copies.append(pltpu.make_async_copy(gate_ref, gate_out, sem.at[13]))
    for d in copies:
        d.start()
    for d in copies:
        d.wait()


def fused_body(layer_input, out_grad, routes, gates, gate_weight, up_weight, down_weight):
    T, C = layer_input.shape[1:]
    D, F = gate_weight.shape[2:]
    K = -(-(3 * T // 4) // 128) * 128
    vmem = pl.BlockSpec(memory_space=pltpu.VMEM)
    hbm = pl.BlockSpec(memory_space=pl.ANY)
    far = pl.BlockSpec(memory_space=pltpu.HBM)
    shape = jax.ShapeDtypeStruct
    rows = (4, 2, K, C)
    chunk = (C // 256, K, 256)
    pair = (C // 256, 2, K, 256)
    last = (C // 256, T, 256)
    ig, gate_grad, gw, uw, dw = pl.pallas_call(
        functools.partial(layer_kernel, T, K, C, F),
        out_shape=(
            shape((T, C), BF16), shape((1, T), F32),
            shape((4, C, F), BF16), shape((4, C, F), BF16), shape((F, D), BF16),
        ),
        in_specs=[far] * 3 + [vmem] + [far] * 3,
        out_specs=(vmem,) * 5,
        scratch_shapes=[
            pltpu.VMEM((1, T), jnp.int32), pltpu.VMEM((2, K, T), BF16), pltpu.VMEM((4, T, C), BF16), pltpu.VMEM((T, C), BF16),
            pltpu.VMEM(rows, BF16), pltpu.VMEM(rows, BF16),
            pltpu.VMEM((2, K, C), BF16), pltpu.VMEM((K, C), BF16),
            pltpu.VMEM((K, 128), BF16), pltpu.VMEM((K, 128), BF16),
            pltpu.VMEM((2 * K, F), F32), pltpu.VMEM((2 * K, F), F32), pltpu.VMEM((2 * K, F), F32),
            pltpu.VMEM((2 * K, F), BF16), pltpu.VMEM((2 * K, F), BF16), pltpu.VMEM((2 * K, F), BF16),
            pltpu.VMEM((2,) + pair, BF16), pltpu.VMEM((2,) + pair, BF16),
            pltpu.VMEM(pair, BF16), pltpu.VMEM(pair, BF16), pltpu.VMEM(pair, BF16),
            pltpu.VMEM(chunk, BF16), pltpu.VMEM(chunk, BF16),
            pltpu.VMEM(last, BF16), pltpu.VMEM(last, BF16),
            pltpu.VMEM((2, 16, K), BF16), pltpu.VMEM((8, 16, K), BF16),
            pltpu.SemaphoreType.DMA((22 + 5 * (C // 256),)),
            pltpu.SemaphoreType.DMA((22 + 5 * (C // 256),)),
            pltpu.SemaphoreType.DMA((6,)),
        ],
        compiler_params=pltpu.CompilerParams(
            collective_id=0, has_side_effects=True, vmem_limit_bytes=41 * 2**20
        ),
        name="layer",
    )(
        layer_input[0], out_grad[0], routes.reshape(1, T), gates.reshape(1, T),
        gate_weight.reshape(4, C, F), up_weight.reshape(4, C, F), down_weight.reshape(F, D),
    )
    ig, gate_grad, gw, uw, dw = pl.pallas_call(
        store_kernel,
        out_shape=(shape((T, C), BF16), shape((1, T), F32), shape((D, F), BF16), shape((D, F), BF16), shape((F, D), BF16)),
        in_specs=[vmem] * 5,
        out_specs=(far,) * 5,
        scratch_shapes=[pltpu.SemaphoreType.DMA((14,))],
        compiler_params=pltpu.CompilerParams(vmem_limit_bytes=16 * 2**20),
        name="store",
    )(ig, gate_grad, gw.reshape(D, F), uw.reshape(D, F), dw)
    return (
        ig[None], gate_grad.reshape(1, T, 1), gw[None, None], uw[None, None], dw[None, None]
    )


def body(*args):
    routes, gate_weight = args[2], args[4]
    small = lax.axis_size("node") == 2 and lax.axis_size("local") == 4
    if small and routes.shape[2] == 1 and gate_weight.shape[1] == 1:
        return fused_body(*args)
    return general_body(*args)


def solution(mesh):
    return jax.shard_map(
        body,
        mesh=mesh,
        in_specs=(
            P("section", "node", "local"),
            P("section", "node", "local"),
            P("section", "node", None),
            P("section", "node", None),
            P("section", "node", None, "local"),
            P("section", "node", None, "local"),
            P("section", "node", "local", None),
        ),
        out_specs=(
            P("section", "node", "local"),
            P("section", "node", None),
            P("section", "node", None, "local"),
            P("section", "node", None, "local"),
            P("section", "node", "local", None),
        ),
        check_vma=False,
    )
```
